256 devices in a mesh: row: 16 (over y, z_lo, core), col: 16 (over x, z_hi).
Axes of the slice: x: 4, y: 4, z: 8 (z_hi: 4, z_lo: 2; z = z_hi * 2 + z_lo), core: 2. Of those that a mesh axis runs over, the one named last changes fastest.
Arguments:
- strips: bfloat16 [16, 16, 4, 1, 2048, 128], P('row', 'col'), may hold values from -6 to 6
- occupancy: int32 [16, 16], replicated, may hold values 0 or 1
Outputs:
- correlations: float32 [16, 16, 8, 128, 128], P('row', 'col')
The draws below stay inside these ranges and needn't reach their ends.
All inputs are finite; a program needn't handle non-finite values.
Results may differ from the reference program's by a relative error of at most 0.0094.
Values may be sent and summed in bfloat16 or wider, within the bound.
A program may use at most 128 MiB of HBM per device.

```python
import math
import jax
import jax.numpy as jnp
from jax import lax

L = 2048
W = 128
PLANES = 1
NR = 16
NC = 16


def touch_ends(drawn, key, smallest, high):
    dims = drawn.shape
    spot = [jax.random.randint(jax.random.fold_in(key, axis), (), 0, dims[axis]) for axis in range(len(dims))]
    drawn = drawn.at[tuple(spot)].set(smallest)
    longest = dims.index(max(dims))
    spot[longest] = (spot[longest] + 1) % dims[longest]
    return drawn.at[tuple(spot)].set(high)


def steps_of(stream_key, shape, shards, smallest, high):
    loudness = 1.0
    for position, shards_of in shards:
        steps = jax.random.uniform(jax.random.fold_in(jax.random.fold_in(stream_key, 6), position), (shards_of,), jnp.float32, smallest / len(shards), high / len(shards))
        loudness = loudness * jnp.repeat(jnp.exp(steps), shape[position] // shards_of).reshape((-1,) + (1,) * (len(shape) - 1 - position))
    return loudness


def centred(own_key, shape, spread, most, cuts=(), dtype=jnp.bfloat16):
    array = jax.random.normal(own_key, shape, jnp.float32) * spread
    if len(cuts) > 0:
        array = steps_of(own_key, shape, cuts, -0.22, 0.18) * array
    return jnp.clip(array, min=-most, max=most).astype(dtype)


def setup_inputs(seed: int = 0) -> dict:
    key_list = jax.random.split(jax.random.key(seed), 3)
    strips = centred(key_list[0], (NR, NC, 4, PLANES, L, W), 1.0, 6.0, ((0, 16), (1, 16)))
    occupancy = touch_ends((jax.random.randint(key_list[1], (NR, NC), 0, 3) < 2).astype(jnp.int32), jax.random.fold_in(key_list[1], 1), 0, 1)
    return dict(strips=strips, occupancy=occupancy)


def table_rows(row_index, length):
    column = lax.iota(jnp.int32, length)
    product = row_index[:, None] * column[None, :] % length
    angle = product.astype(jnp.float32) * (2.0 * math.pi / length)
    return (jnp.cos(angle).astype(jnp.bfloat16), jnp.sin(angle).astype(jnp.bfloat16))

def spin_matrix(breadth, forward):
    cosine, sine_table = table_rows(lax.iota(jnp.int32, breadth), breadth)
    upper_right = -sine_table if forward else sine_table
    return jnp.concatenate([jnp.concatenate([cosine, upper_right], 1), jnp.concatenate([-upper_right, cosine], 1)], 0)

def along_length(flattened, length, row_block):
    real_parts = []
    imag_parts = []
    for first_row in range(0, length, row_block):
        cosine, sine_table = table_rows(lax.iota(jnp.int32, row_block) + first_row, length)
        real_parts.append(jnp.dot(cosine, flattened, preferred_element_type=jnp.float32))
        imag_parts.append(-jnp.dot(sine_table, flattened, preferred_element_type=jnp.float32))
    return (jnp.concatenate(real_parts, 0).astype(jnp.bfloat16), jnp.concatenate(imag_parts, 0).astype(jnp.bfloat16))

def transform(pieces, row_block):
    planes, length, breadth = pieces[0].shape
    joined = jnp.concatenate(pieces, 0)
    pieces_count = joined.shape[0]
    flattened = jnp.transpose(joined, (1, 0, 2)).reshape(length, pieces_count * breadth)
    real_part, imag_part = along_length(flattened, length, row_block)
    halves = jnp.concatenate([real_part.reshape(length, pieces_count, breadth), imag_part.reshape(length, pieces_count, breadth)], 2)
    spectrum = jnp.einsum('nqc,cd->nqd', halves.astype(jnp.float32), spin_matrix(breadth, True).astype(jnp.float32)).astype(jnp.bfloat16)
    return [spectrum[:, k * planes:(k + 1) * planes] for k in range(len(pieces))]

def correlate(left_spec, right_spec, row_index):
    length, planes, doubled = left_spec.shape
    breadth = doubled // 2
    left_full = left_spec.astype(jnp.float32)
    right_full = right_spec.astype(jnp.float32)
    real_left, imag_left = (left_full[..., :breadth], left_full[..., breadth:])
    real_right, imag_right = (right_full[..., :breadth], right_full[..., breadth:])
    cross_real = real_left * real_right + imag_left * imag_right
    cross_imag = imag_left * real_right - real_left * imag_right
    magnitude = jnp.sqrt(cross_real * cross_real + cross_imag * cross_imag)
    lower_bound = 0.5 * lax.optimization_barrier(jnp.mean(magnitude, axis=(0, 2), keepdims=True)) + 1e-06
    inverse_size = 1.0 / jnp.maximum(magnitude, lower_bound)
    summed = jnp.concatenate([lax.optimization_barrier(jnp.sum(cross_real * inverse_size, axis=1)), lax.optimization_barrier(jnp.sum(cross_imag * inverse_size, axis=1))], 1).astype(jnp.bfloat16)
    partial_back = jnp.dot(summed, spin_matrix(breadth, False), preferred_element_type=jnp.float32).astype(jnp.bfloat16)
    cosine, sine_table = table_rows(row_index, length)
    weights = jnp.concatenate([cosine, -sine_table], 1)
    stacked = jnp.concatenate([partial_back[:, :breadth], partial_back[:, breadth:]], 0)
    return jnp.dot(weights, stacked, preferred_element_type=jnp.float32) / (planes * math.sqrt(length * breadth))

def pair_map(left_strip, right_strip, row_index):
    spectra = transform([left_strip, right_strip], left_strip.shape[1])
    return correlate(spectra[0], spectra[1], row_index)

def reference(strips, occupancy):
    planes, length, breadth = strips.shape[3:]
    edge_rows = (lax.iota(jnp.int32, breadth) - breadth // 2) % length
    corner_rows = lax.iota(jnp.int32, breadth)

    def pair_grid(left_strips, right_strips, row_index):
        leading = left_strips.shape[:2]
        flattened = (left_strips.reshape((-1,) + left_strips.shape[2:]), right_strips.reshape((-1,) + right_strips.shape[2:]))
        results = lax.map(lambda couple: pair_map(couple[0], couple[1], row_index), flattened)
        return results.reshape(leading + results.shape[1:])
    occupied = occupancy.astype(jnp.float32)
    east_maps = pair_grid(strips[:, :-1, 0], strips[:, 1:, 1], edge_rows)
    east_maps = east_maps * (occupied[:, :-1] * occupied[:, 1:])[:, :, None, None]
    south_maps = pair_grid(strips[:-1, :, 2], strips[1:, :, 3], edge_rows)
    south_maps = south_maps * (occupied[:-1, :] * occupied[1:, :])[:, :, None, None]
    down_right = pair_grid(strips[:-1, :-1, 0, :, length - breadth:], strips[1:, 1:, 1, :, :breadth], corner_rows)
    down_right = down_right * (occupied[:-1, :-1] * occupied[1:, 1:])[:, :, None, None]
    down_left = pair_grid(strips[:-1, 1:, 1, :, length - breadth:], strips[1:, :-1, 0, :, :breadth], corner_rows)
    down_left = down_left * (occupied[:-1, 1:] * occupied[1:, :-1])[:, :, None, None]

    def place_maps(results, rows_pad, cols_pad):
        return jnp.pad(results, (rows_pad, cols_pad, (0, 0), (0, 0)))
    return jnp.stack([place_maps(east_maps, (0, 0), (0, 1)), place_maps(south_maps, (0, 1), (0, 0)), place_maps(down_right, (0, 1), (0, 1)), place_maps(down_left, (0, 1), (1, 0)), place_maps(east_maps, (0, 0), (1, 0)), place_maps(south_maps, (1, 0), (0, 0)), place_maps(down_right, (1, 0), (1, 0)), place_maps(down_left, (1, 0), (0, 1))], 2)
```

```python
import functools
import math

import jax
import jax.numpy as jnp
import ml_dtypes
import numpy as np
from jax import lax
from jax.experimental import pallas as pl
from jax.experimental.pallas import tpu as pltpu
from jax.sharding import PartitionSpec as P

MESH = pl.DeviceIdType.MESH
CHUNK = 256
BF16 = jnp.bfloat16
F32 = jnp.float32


def trig(rows, columns, length):
    product = (rows[:, None].astype(np.int64) * columns[None, :]) % length
    angle = (product.astype(np.float32) * np.float32(2.0 * math.pi / length)).astype(np.float64)
    return np.cos(angle), np.sin(angle)


def half_rows(length):
    return -(-(length // 2 + 1) // 16) * 16


def forward_table(length):
    rows = np.arange(half_rows(length))
    cosine, sine = trig(rows, np.arange(length), length)
    keep = (rows <= length // 2)[:, None]
    return np.concatenate([cosine * keep, -sine * keep], 0).astype(ml_dtypes.bfloat16)


def inverse_table(shifts, length):
    rows = np.arange(half_rows(length))
    weight = np.where((rows == 0) | (rows == length // 2), 1.0, 2.0) * (rows <= length // 2)
    cosine, sine = trig(shifts % length, rows, length)
    cosine = cosine.astype(ml_dtypes.bfloat16).astype(np.float64)
    sine = sine.astype(ml_dtypes.bfloat16).astype(np.float64)
    return np.concatenate([cosine * weight, -sine * weight], 1).astype(ml_dtypes.bfloat16)


def spin(breadth):
    cosine, sine = trig(np.arange(breadth), np.arange(breadth), breadth)
    forward = np.block([[cosine, -sine], [sine, cosine]])
    back = np.block([[cosine, sine], [-sine, cosine]])
    return np.stack([forward, back]).astype(ml_dtypes.bfloat16)


def kernel(
    rows, cols, length, breadth,
    strips, occ, table, inverse, corner_table, corner_inverse, spins, out,
    tab, inv_tab, ctab, cinv_tab, spin_v, occ_s, own, got, corner_own, corner_got,
    acc, g_re, g_im, g_inv, z_all, map_out, map_in, out_v,
    tab_sem, small_sem, own_sem, corner_sem, send_sem, recv_sem,
    csend_sem, crecv_sem, msend_sem, mrecv_sem, out_sem,
):
    chunks = length // CHUNK
    half = half_rows(length)
    chalf = half_rows(breadth)
    row = lax.axis_index("row")
    col = lax.axis_index("col")
    parity = lax.rem(row, 2)
    up, down = lax.rem(row + rows - 1, rows), lax.rem(row + 1, rows)
    left, right = lax.rem(col + cols - 1, cols), lax.rem(col + 1, cols)

    barrier = pltpu.get_barrier_semaphore()
    neighbours = [
        (up, left), (up, col), (up, right), (row, left),
        (row, right), (down, left), (down, col), (down, right),
    ]
    for neighbour in neighbours:
        pl.semaphore_signal(barrier, inc=1, device_id=neighbour, device_id_type=MESH)

    small = [
        pltpu.make_async_copy(corner_table, ctab, small_sem.at[0]),
        pltpu.make_async_copy(spins, spin_v, small_sem.at[1]),
        pltpu.make_async_copy(corner_inverse, cinv_tab, small_sem.at[2]),
        pltpu.make_async_copy(inverse, inv_tab, small_sem.at[3]),
        pltpu.make_async_copy(occ, occ_s, small_sem.at[4]),
    ]
    low = pl.ds(length - breadth, breadth)
    top = pl.ds(0, breadth)
    corner_places = [(0, low), (1, low), (1, top), (0, top)]
    corner_loads = [
        pltpu.make_async_copy(strips.at[s, place], corner_own.at[k], corner_sem.at[k])
        for k, (s, place) in enumerate(corner_places)
    ]
    own_loads = [
        pltpu.make_async_copy(strips.at[2], own.at[0], own_sem.at[0]),
        pltpu.make_async_copy(strips.at[parity], own.at[1], own_sem.at[1]),
    ]

    def table_load(c):
        return pltpu.make_async_copy(table.at[c], tab.at[c], tab_sem.at[c])

    for copy in small + corner_loads + own_loads:
        copy.start()
    for c in range(chunks):
        table_load(c).start()

    pl.semaphore_wait(barrier, len(neighbours))

    side = jnp.where(parity == 0, left, right)
    other_side = jnp.where(parity == 0, right, left)

    def strip_copy(idx, c):
        piece = pl.ds(c * CHUNK if isinstance(c, int) else pl.multiple_of(c * CHUNK, CHUNK), CHUNK)
        source = jnp.where(idx == 0, 3, 1 - parity)
        target = (jnp.where(idx == 0, up, row), jnp.where(idx == 0, col, side))
        return pltpu.make_async_remote_copy(
            src_ref=strips.at[source, piece],
            dst_ref=got.at[idx, piece],
            send_sem=send_sem.at[idx, c],
            recv_sem=recv_sem.at[idx, c],
            device_id=target,
            device_id_type=MESH,
        )

    def corner_copy(k):
        target = [(down, right), (down, left), (up, left), (up, right)][k]
        s, place = corner_places[k]
        return pltpu.make_async_remote_copy(
            src_ref=strips.at[s, place],
            dst_ref=corner_got.at[(k + 2) % 4],
            send_sem=csend_sem.at[k],
            recv_sem=crecv_sem.at[(k + 2) % 4],
            device_id=target,
            device_id_type=MESH,
        )

    for k in range(4):
        corner_copy(k).start()
    for idx in (1, 0):
        def start(c, carry, idx=idx):
            strip_copy(idx, c).start()
            return carry
        lax.fori_loop(0, chunks, start, 0)

    for copy in small:
        copy.wait()

    def alive(r1, c1, dr, dc):
        r2, c2 = r1 + dr, c1 + dc
        inside = (r2 >= 0) & (r2 < rows) & (c2 >= 0) & (c2 < cols)
        second = occ_s[lax.rem(r2 + rows, rows), lax.rem(c2 + cols, cols)]
        return (occ_s[r1, c1] * second * jnp.where(inside, 1, 0)).astype(F32)


    def correlate(base, size, block, n, sign, inv_ref, shift_count):
        steps = size // block

        def cross(b, total):
            at = pl.multiple_of(b * block, block)
            c_part = acc[pl.ds(base + at, block), :]
            s_part = acc[pl.ds(base + size + at, block), :]
            halves = jnp.concatenate(
                [
                    jnp.concatenate([c_part[:, :breadth], s_part[:, :breadth]], 1),
                    jnp.concatenate([c_part[:, breadth:], s_part[:, breadth:]], 1),
                ],
                0,
            ).astype(BF16)
            y = jnp.dot(halves, spin_v[0], preferred_element_type=F32).astype(BF16).astype(F32)
            a_re, a_im = y[:block, :breadth], y[:block, breadth:]
            b_re, b_im = y[block:, :breadth], y[block:, breadth:]
            re = a_re * b_re + a_im * b_im
            im = a_im * b_re - a_re * b_im
            square = re * re + im * im
            inverse_m = lax.rsqrt(jnp.maximum(square, 1e-36))
            g_re[pl.ds(at, block), :] = re
            g_im[pl.ds(at, block), :] = im
            g_inv[pl.ds(at, block), :] = inverse_m
            k = lax.broadcasted_iota(jnp.int32, (block, breadth), 0) + at
            weight = jnp.where((k == 0) | (k == n // 2), 1.0, 2.0)
            m = square * inverse_m * weight
            return total + jnp.sum(m.reshape(block // 8, 8, breadth), 0)

        total = lax.fori_loop(0, steps, cross, jnp.zeros((8, breadth), F32))
        floor = 0.5 * (jnp.sum(total, keepdims=True) / (n * breadth)) + 1e-6
        most = 1.0 / floor

        def back(b, carry):
            at = pl.multiple_of(b * block, block)
            scale = jnp.minimum(g_inv[pl.ds(at, block), :], most)
            r = jnp.concatenate(
                [g_re[pl.ds(at, block), :] * scale, g_im[pl.ds(at, block), :] * (scale * sign)], 1
            ).astype(BF16)
            z = jnp.dot(r, spin_v[1], preferred_element_type=F32).astype(BF16)
            z_all[pl.ds(at, block), :] = z[:, :breadth]
            z_all[pl.ds(size + at, block), :] = z[:, breadth:]
            return carry

        lax.fori_loop(0, steps, back, 0)
        return jnp.dot(inv_ref[...], z_all[pl.ds(0, 2 * size), :], preferred_element_type=F32)

    def length_step(idx, c, first):
        piece = pl.ds(c * CHUNK if isinstance(c, int) else pl.multiple_of(c * CHUNK, CHUNK), CHUNK)
        strip_copy(idx, c).wait_recv()
        x = jnp.concatenate([own[idx, piece, :], got[idx, piece, :]], 1)
        rows_at = 2 * half // 5

        def part(b, carry):
            at = pl.ds(pl.multiple_of(b * rows_at, 16), rows_at)
            product = jnp.dot(tab[c, at, :], x, preferred_element_type=F32)
            if first:
                acc[at, :] = product
            else:
                acc[at, :] += product
            return carry

        lax.fori_loop(0, 5, part, 0)

    def corners():
        scale = 1.0 / math.sqrt(breadth * breadth)
        steps = [(1, 1), (1, -1), (-1, -1), (-1, 1)]
        for k in range(4):
            corner_loads[k].wait()
            corner_copy((k + 2) % 4).wait_recv()
            x = jnp.concatenate([corner_own[k], corner_got[k]], 1)
            acc[pl.ds(0, 2 * chalf), :] = jnp.dot(ctab[...], x, preferred_element_type=F32)
            result = correlate(0, chalf, chalf, breadth, 1.0 if k < 2 else -1.0, cinv_tab, breadth)
            slot = (2, 3, 6, 7)[k]
            out_v[slot] = result * (alive(row, col, *steps[k]) * scale)
            out_copy(slot).start()

    def out_copy(slot):
        return pltpu.make_async_copy(out_v.at[slot], out.at[slot], out_sem.at[slot])

    def map_copy(idx):
        target = (jnp.where(idx == 0, down, row), jnp.where(idx == 0, col, other_side))
        return pltpu.make_async_remote_copy(
            src_ref=map_out.at[idx],
            dst_ref=map_in.at[idx],
            send_sem=msend_sem.at[idx],
            recv_sem=mrecv_sem.at[idx],
            device_id=target,
            device_id_type=MESH,
        )

    for copy in own_loads:
        copy.wait()

    def phase(p, carry):
        idx = lax.rem(p + parity, 2)

        @pl.when(p == 0)
        def _():
            table_load(0).wait()

        length_step(idx, 0, True)

        def more(c, inner):
            @pl.when(p == 0)
            def _():
                table_load(c).wait()

            length_step(idx, c, False)
            return inner

        lax.fori_loop(1, chunks, more, 0)
        sign = jnp.where(idx == 0, 1, 1 - 2 * parity).astype(F32)
        result = correlate(0, half, half // 5, length, sign, inv_tab, breadth)
        live = alive(
            row, col, jnp.where(idx == 0, 1, 0), jnp.where(idx == 0, 0, 1 - 2 * parity)
        )
        result = result * (live * (1.0 / math.sqrt(length * breadth)))
        map_out[idx] = result.astype(BF16)
        map_copy(idx).start()
        slot = jnp.where(idx == 0, 1, 4 * parity)
        out_v[slot] = result
        out_copy(slot).start()

        @pl.when(p == 0)
        def _():
            corners()

        return carry

    lax.fori_loop(0, 2, phase, 0)

    for idx in (1, 0):
        map_copy(idx).wait_recv()
        slot = 4 * (1 - parity) if idx == 1 else 5
        out_v[slot] = map_in[idx].astype(F32)
        out_copy(slot).start()

    for idx in (1, 0):
        map_copy(idx).wait_send()

        def sent(c, carry, idx=idx):
            strip_copy(idx, c).wait_send()
            return carry

        lax.fori_loop(0, chunks, sent, 0)
    for k in range(4):
        corner_copy(k).wait_send()
    for slot in range(8):
        out_copy(slot).wait()


def per_device(rows, cols, strips, occupancy):
    length, breadth = strips.shape[4:]
    chunks = length // CHUNK
    half, chalf = half_rows(length), half_rows(breadth)
    forward = forward_table(length)
    table = jnp.asarray(
        np.ascontiguousarray(forward.reshape(2 * half, chunks, CHUNK).transpose(1, 0, 2))
    )
    inverse = jnp.asarray(inverse_table(np.arange(breadth) - breadth // 2, length))
    corner_table = jnp.asarray(forward_table(breadth))
    corner_inverse = jnp.asarray(inverse_table(np.arange(breadth), breadth))
    spins = jnp.asarray(spin(breadth))
    hbm = pl.BlockSpec(memory_space=pl.ANY)
    dma = pltpu.SemaphoreType.DMA
    result = pl.pallas_call(
        functools.partial(kernel, rows, cols, length, breadth),
        out_shape=jax.ShapeDtypeStruct((8, breadth, breadth), F32),
        in_specs=[hbm] * 7,
        out_specs=hbm,
        scratch_shapes=[
            pltpu.VMEM((chunks, 2 * half, CHUNK), BF16),
            pltpu.VMEM((breadth, 2 * half), BF16),
            pltpu.VMEM((2 * chalf, breadth), BF16),
            pltpu.VMEM((breadth, 2 * chalf), BF16),
            pltpu.VMEM((2, 2 * breadth, 2 * breadth), BF16),
            pltpu.SMEM((rows, cols), jnp.int32),
            pltpu.VMEM((2, length, breadth), BF16),
            pltpu.VMEM((2, length, breadth), BF16),
            pltpu.VMEM((4, breadth, breadth), BF16),
            pltpu.VMEM((4, breadth, breadth), BF16),
            pltpu.VMEM((2 * half, 2 * breadth), F32),
            pltpu.VMEM((half, breadth), F32),
            pltpu.VMEM((half, breadth), F32),
            pltpu.VMEM((half, breadth), F32),
            pltpu.VMEM((2 * half, breadth), BF16),
            pltpu.VMEM((2, breadth, breadth), BF16),
            pltpu.VMEM((2, breadth, breadth), BF16),
            pltpu.VMEM((8, breadth, breadth), F32),
            dma((chunks,)),
            dma((5,)),
            dma((2,)),
            dma((4,)),
            dma((2, chunks)),
            dma((2, chunks)),
            dma((4,)),
            dma((4,)),
            dma((2,)),
            dma((2,)),
            dma((8,)),
        ],
        compiler_params=pltpu.CompilerParams(
            collective_id=0, has_side_effects=True, vmem_limit_bytes=40 * 1024 * 1024
        ),
    )(
        strips.reshape(4, length, breadth), occupancy, table, inverse, corner_table,
        corner_inverse, spins,
    )
    return result[None, None]


def solution(mesh):
    rows, cols = mesh.shape["row"], mesh.shape["col"]
    return jax.shard_map(
        functools.partial(per_device, rows, cols),
        mesh=mesh,
        in_specs=(P("row", "col", None, None, None, None), P()),
        out_specs=P("row", "col", None, None, None),
        check_vma=False,
    )
```

```python
import functools
import math

import jax
import jax.numpy as jnp
import ml_dtypes
import numpy as np
from jax import lax
from jax.experimental import pallas as pl
from jax.experimental.pallas import tpu as pltpu
from jax.sharding import PartitionSpec as P

MESH = pl.DeviceIdType.MESH
CHUNK = 512
WIDE = 256
BLOCKS = 5
BF16 = jnp.bfloat16
F32 = jnp.float32


def trig(rows, columns, length):
    product = (rows[:, None].astype(np.int64) * columns[None, :]) % length
    angle = (product.astype(np.float32) * np.float32(2.0 * math.pi / length)).astype(np.float64)
    return np.cos(angle), np.sin(angle)


def half_rows(length):
    return -(-(length // 2 + 1) // 16) * 16


def forward_table(length):
    rows = np.arange(half_rows(length))
    cosine, sine = trig(rows, np.arange(length), length)
    keep = (rows <= length // 2)[:, None]
    return np.concatenate([cosine * keep, -sine * keep], 0).astype(ml_dtypes.bfloat16)


def inverse_table(shifts, length):
    rows = np.arange(half_rows(length))
    weight = np.where((rows == 0) | (rows == length // 2), 1.0, 2.0) * (rows <= length // 2)
    cosine, sine = trig(shifts % length, rows, length)
    cosine = cosine.astype(ml_dtypes.bfloat16).astype(np.float64)
    sine = sine.astype(ml_dtypes.bfloat16).astype(np.float64)
    return np.concatenate([cosine * weight, -sine * weight], 1).astype(ml_dtypes.bfloat16)


def spin(breadth):
    cosine, sine = trig(np.arange(breadth), np.arange(breadth), breadth)
    forward = np.block([[cosine, -sine], [sine, cosine]])
    back = np.block([[cosine, sine], [-sine, cosine]])
    return np.stack([forward, back]).astype(ml_dtypes.bfloat16)


def table_places(length, breadth):
    sizes = [
        (length // WIDE) * 2 * half_rows(length),
        4 * breadth,
        -(-2 * half_rows(length) // WIDE) * breadth,
        2 * half_rows(breadth),
        breadth,
    ]
    return [(sum(sizes[:k]), size) for k, size in enumerate(sizes)]


def packed_tables(length, breadth):
    def blocks(array):
        rows, columns = array.shape
        array = np.pad(array, ((0, 0), (0, -columns % WIDE)))
        return array.reshape(rows, -1, WIDE).transpose(1, 0, 2).reshape(-1, WIDE)

    parts = [
        forward_table(length),
        spin(breadth).reshape(4 * breadth, 2 * breadth),
        inverse_table(np.arange(breadth) - breadth // 2, length),
        forward_table(breadth),
        inverse_table(np.arange(breadth), breadth),
    ]
    return np.concatenate([blocks(part) for part in parts], 0)


def kernel(
    rows, cols, length, breadth,
    strips, occ, tables, out,
    tab, inv_tab, ctab, cinv_tab, spin_v, occ_s, own, got, corner_own, corner_got,
    acc, g_re, g_im, g_inv, z_all, map_out, map_in, out_v,
    tab_sem, small_sem, own_sem, corner_sem, send_sem, recv_sem,
    csend_sem, crecv_sem, msend_sem, mrecv_sem, out_sem,
):
    chunks = length // CHUNK
    half = half_rows(length)
    chalf = half_rows(breadth)
    row = lax.axis_index("row")
    col = lax.axis_index("col")
    parity = lax.rem(row, 2)
    up, down = lax.rem(row + rows - 1, rows), lax.rem(row + 1, rows)
    left, right = lax.rem(col + cols - 1, cols), lax.rem(col + 1, cols)

    barrier = pltpu.get_barrier_semaphore()
    neighbours = [
        (up, left), (up, col), (up, right), (row, left),
        (row, right), (down, left), (down, col), (down, right),
    ]
    for neighbour in neighbours:
        pl.semaphore_signal(barrier, inc=1, device_id=neighbour, device_id_type=MESH)

    places = table_places(length, breadth)
    small = [
        pltpu.make_async_copy(tables.at[pl.ds(*places[k + 1])], dest, small_sem.at[k])
        for k, dest in enumerate((spin_v, inv_tab, ctab, cinv_tab))
    ]
    small.append(pltpu.make_async_copy(occ, occ_s, small_sem.at[4]))
    low = pl.ds(length - breadth, breadth)
    top = pl.ds(0, breadth)
    corner_places = [(0, low), (1, low), (1, top), (0, top)]
    corner_loads = [
        pltpu.make_async_copy(strips.at[s, place], corner_own.at[k], corner_sem.at[k])
        for k, (s, place) in enumerate(corner_places)
    ]
    own_loads = [
        pltpu.make_async_copy(strips.at[2], own.at[0], own_sem.at[0]),
        pltpu.make_async_copy(strips.at[parity], own.at[1], own_sem.at[1]),
    ]

    def table_load(c):
        at = pl.multiple_of(c * (2 * half), 16)
        return pltpu.make_async_copy(
            tables.at[pl.ds(at, 2 * half)], tab.at[c], tab_sem.at[c]
        )

    for copy in small + corner_loads + own_loads:
        copy.start()
    for c in range(length // WIDE):
        table_load(c).start()

    pl.semaphore_wait(barrier, len(neighbours))

    side = jnp.where(parity == 0, left, right)
    other_side = jnp.where(parity == 0, right, left)

    def strip_copy(idx, c):
        piece = pl.ds(c * CHUNK if isinstance(c, int) else pl.multiple_of(c * CHUNK, CHUNK), CHUNK)
        source = jnp.where(idx == 0, 3, 1 - parity)
        target = (jnp.where(idx == 0, up, row), jnp.where(idx == 0, col, side))
        return pltpu.make_async_remote_copy(
            src_ref=strips.at[source, piece],
            dst_ref=got.at[idx, piece],
            send_sem=send_sem.at[idx, c],
            recv_sem=recv_sem.at[idx, c],
            device_id=target,
            device_id_type=MESH,
        )

    def corner_copy(k):
        target = [(down, right), (down, left), (up, left), (up, right)][k]
        s, place = corner_places[k]
        return pltpu.make_async_remote_copy(
            src_ref=strips.at[s, place],
            dst_ref=corner_got.at[(k + 2) % 4],
            send_sem=csend_sem.at[k],
            recv_sem=crecv_sem.at[(k + 2) % 4],
            device_id=target,
            device_id_type=MESH,
        )

    for k in range(4):
        corner_copy(k).start()
    def send(idx):
        def start(c, carry):
            strip_copy(idx, c).start()
            return carry

        lax.fori_loop(0, chunks, start, 0)

    send(1)

    @pl.when(parity == 1)
    def _():
        send(0)

    for copy in small:
        copy.wait()

    def alive(r1, c1, dr, dc):
        r2, c2 = r1 + dr, c1 + dc
        inside = (r2 >= 0) & (r2 < rows) & (c2 >= 0) & (c2 < cols)
        second = occ_s[lax.rem(r2 + rows, rows), lax.rem(c2 + cols, cols)]
        return (occ_s[r1, c1] * second * jnp.where(inside, 1, 0)).astype(F32)


    def cross(c_part, s_part, n, first_row):
        size = c_part.shape[0]
        halves = jnp.concatenate(
            [
                jnp.concatenate([c_part[:, :breadth], s_part[:, :breadth]], 1),
                jnp.concatenate([c_part[:, breadth:], s_part[:, breadth:]], 1),
            ],
            0,
        ).astype(BF16)
        y = jnp.dot(halves, spin_v[: 2 * breadth, :], preferred_element_type=F32).astype(BF16).astype(F32)
        a_re, a_im = y[:size, :breadth], y[:size, breadth:]
        b_re, b_im = y[size:, :breadth], y[size:, breadth:]
        re = a_re * b_re + a_im * b_im
        im = a_im * b_re - a_re * b_im
        square = re * re + im * im
        inverse_m = lax.rsqrt(jnp.maximum(square, 1e-36))
        m = square * inverse_m
        first = lax.broadcasted_iota(jnp.int32, (8, breadth), 0)
        total = jnp.zeros((8, breadth), F32)
        for at in range(0, size, 8):
            part = m[at : at + 8]
            if first_row + at == 0 or first_row + at == n // 2:
                part = part * jnp.where(first == 0, 0.5, 1.0)
            total = total + part
        return re, im, inverse_m, total

    def limit_of(total, n):
        floor = 0.5 * (jnp.sum(total, keepdims=True) * (2.0 / (n * breadth))) + 1e-6
        return 1.0 / floor

    def back(re, im, inverse_m, most, sign):
        scale = jnp.minimum(inverse_m, most)
        r = jnp.concatenate([re * scale, im * (scale * sign)], 1).astype(BF16)
        return jnp.dot(r, spin_v[2 * breadth :, :], preferred_element_type=F32).astype(BF16)

    def edge_map(sign):
        block = half // BLOCKS
        total = jnp.zeros((8, breadth), F32)
        for at in range(0, half, block):
            re, im, inverse_m, part = cross(
                acc[pl.ds(at, block), :], acc[pl.ds(half + at, block), :], length, at
            )
            here = pl.ds(at, block)
            g_re[here, :], g_im[here, :], g_inv[here, :] = re, im, inverse_m
            total = total + part
        most = limit_of(total, length)
        inv = jnp.concatenate(
            [inv_tab[pl.ds(at, breadth), :] for at in range(0, inv_tab.shape[0], breadth)], 1
        )[:, : 2 * half]
        for at in range(0, half, block):
            here = pl.ds(at, block)
            z = back(g_re[here, :], g_im[here, :], g_inv[here, :], most, sign)
            z_all[here, :] = z[:, :breadth]
            z_all[pl.ds(half + at, block), :] = z[:, breadth:]
        return jnp.dot(inv, z_all[...], preferred_element_type=F32)

    def length_step(idx, c, first):
        piece = pl.ds(c * CHUNK if isinstance(c, int) else pl.multiple_of(c * CHUNK, CHUNK), CHUNK)
        strip_copy(idx, c).wait_recv()
        x = jnp.concatenate([own[idx, piece, :], got[idx, piece, :]], 1)
        step = jnp.concatenate(
            [tab[c * (CHUNK // WIDE) + k] for k in range(CHUNK // WIDE)], 1
        )
        product = jnp.dot(step, x, preferred_element_type=F32)
        if first:
            acc[...] = product
        else:
            acc[...] += product

    def corners():
        scale = 1.0 / math.sqrt(breadth * breadth)
        steps = [(1, 1), (1, -1), (-1, -1), (-1, 1)]
        for k in range(4):
            corner_loads[k].wait()
            corner_copy((k + 2) % 4).wait_recv()
        x = jnp.concatenate(
            [part for k in range(4) for part in (corner_own[k], corner_got[k])], 1
        )
        product = jnp.dot(ctab[:, :breadth], x, preferred_element_type=F32)
        parts = []
        for k in range(4):
            wide = product[:, 2 * breadth * k : 2 * breadth * (k + 1)]
            re, im, inverse_m, total = cross(wide[:chalf], wide[chalf:], breadth, 0)
            z = back(re, im, inverse_m, limit_of(total, breadth), 1.0 if k < 2 else -1.0)
            parts.append(jnp.concatenate([z[:, :breadth], z[:, breadth:]], 0))
        maps = jnp.dot(cinv_tab[:, : 2 * chalf], jnp.concatenate(parts, 1), preferred_element_type=F32)
        for k in range(4):
            slot = (2, 3, 6, 7)[k]
            out_v[slot] = maps[:, breadth * k : breadth * (k + 1)] * (
                alive(row, col, *steps[k]) * scale
            )
            out_copy(slot).start()

    def out_copy(slot):
        return pltpu.make_async_copy(out_v.at[slot], out.at[slot], out_sem.at[slot])

    def map_copy(idx):
        target = (jnp.where(idx == 0, down, row), jnp.where(idx == 0, col, other_side))
        return pltpu.make_async_remote_copy(
            src_ref=map_out.at[idx],
            dst_ref=map_in.at[idx],
            send_sem=msend_sem.at[idx],
            recv_sem=mrecv_sem.at[idx],
            device_id=target,
            device_id_type=MESH,
        )

    for copy in own_loads:
        copy.wait()

    corners()

    @pl.when(parity == 0)
    def _():
        send(0)

    def phase(p, carry):
        idx = lax.rem(p + parity, 2)

        @pl.when(p == 0)
        def _():
            for k in range(CHUNK // WIDE):
                table_load(k).wait()

        length_step(idx, 0, True)

        def more(c, inner):
            @pl.when(p == 0)
            def _():
                for k in range(CHUNK // WIDE):
                    table_load(c * (CHUNK // WIDE) + k).wait()

            length_step(idx, c, False)
            return inner

        lax.fori_loop(1, chunks, more, 0)
        sign = jnp.where(idx == 0, 1, 1 - 2 * parity).astype(F32)
        result = edge_map(sign)
        live = alive(
            row, col, jnp.where(idx == 0, 1, 0), jnp.where(idx == 0, 0, 1 - 2 * parity)
        )
        result = result * (live * (1.0 / math.sqrt(length * breadth)))
        map_out[idx] = result.astype(BF16)
        map_copy(idx).start()
        slot = jnp.where(idx == 0, 1, 4 * parity)
        out_v[slot] = result
        out_copy(slot).start()
        return carry

    lax.fori_loop(0, 2, phase, 0)

    for idx in (1, 0):
        map_copy(idx).wait_recv()
        slot = 4 * (1 - parity) if idx == 1 else 5
        out_v[slot] = map_in[idx].astype(F32)
        out_copy(slot).start()

    for idx in (1, 0):
        map_copy(idx).wait_send()

        def sent(c, carry, idx=idx):
            strip_copy(idx, c).wait_send()
            return carry

        lax.fori_loop(0, chunks, sent, 0)
    for k in range(4):
        corner_copy(k).wait_send()
    for slot in range(8):
        out_copy(slot).wait()


def per_device(rows, cols, strips, occupancy):
    length, breadth = strips.shape[4:]
    chunks = length // CHUNK
    half, chalf = half_rows(length), half_rows(breadth)
    tables = jnp.asarray(packed_tables(length, breadth))
    places = table_places(length, breadth)
    hbm = pl.BlockSpec(memory_space=pltpu.HBM)
    dma = pltpu.SemaphoreType.DMA
    result = pl.pallas_call(
        functools.partial(kernel, rows, cols, length, breadth),
        out_shape=jax.ShapeDtypeStruct((8, breadth, breadth), F32),
        in_specs=[hbm] * 3,
        out_specs=hbm,
        scratch_shapes=[
            pltpu.VMEM((length // WIDE, 2 * half, WIDE), BF16),
            pltpu.VMEM((places[2][1], WIDE), BF16),
            pltpu.VMEM((places[3][1], WIDE), BF16),
            pltpu.VMEM((places[4][1], WIDE), BF16),
            pltpu.VMEM((places[1][1], WIDE), BF16),
            pltpu.SMEM((rows, cols), jnp.int32),
            pltpu.VMEM((2, length, breadth), BF16),
            pltpu.VMEM((2, length, breadth), BF16),
            pltpu.VMEM((4, breadth, breadth), BF16),
            pltpu.VMEM((4, breadth, breadth), BF16),
            pltpu.VMEM((2 * half, 2 * breadth), F32),
            pltpu.VMEM((half, breadth), F32),
            pltpu.VMEM((half, breadth), F32),
            pltpu.VMEM((half, breadth), F32),
            pltpu.VMEM((2 * half, breadth), BF16),
            pltpu.VMEM((2, breadth, breadth), BF16),
            pltpu.VMEM((2, breadth, breadth), BF16),
            pltpu.VMEM((8, breadth, breadth), F32),
            dma((length // WIDE,)),
            dma((5,)),
            dma((2,)),
            dma((4,)),
            dma((2, chunks)),
            dma((2, chunks)),
            dma((4,)),
            dma((4,)),
            dma((2,)),
            dma((2,)),
            dma((8,)),
        ],
        compiler_params=pltpu.CompilerParams(
            collective_id=0, has_side_effects=True, vmem_limit_bytes=54500 * 1024
        ),
    )(strips.reshape(4, length, breadth), occupancy, tables)
    return result[None, None]


def solution(mesh):
    rows, cols = mesh.shape["row"], mesh.shape["col"]
    return jax.shard_map(
        functools.partial(per_device, rows, cols),
        mesh=mesh,
        in_specs=(P("row", "col", None, None, None, None), P()),
        out_specs=P("row", "col", None, None, None),
        check_vma=False,
    )
```

```python
import functools
import math

import jax
import jax.numpy as jnp
import ml_dtypes
import numpy as np
from jax import lax
from jax.experimental import pallas as pl
from jax.experimental.pallas import tpu as pltpu
from jax.sharding import PartitionSpec as P

MESH = pl.DeviceIdType.MESH
CHUNK = 512
WIDE = 256
BLOCKS = 5
BF16 = jnp.bfloat16
F32 = jnp.float32


def trig(rows, columns, length):
    product = (rows[:, None].astype(np.int64) * columns[None, :]) % length
    angle = (product.astype(np.float32) * np.float32(2.0 * math.pi / length)).astype(np.float64)
    return np.cos(angle), np.sin(angle)


def half_rows(length):
    return -(-(length // 2 + 1) // 16) * 16


def forward_table(length):
    rows = np.arange(half_rows(length))
    cosine, sine = trig(rows, np.arange(length), length)
    keep = (rows <= length // 2)[:, None]
    return np.concatenate([cosine * keep, -sine * keep], 0).astype(ml_dtypes.bfloat16)


def inverse_table(shifts, length):
    rows = np.arange(half_rows(length))
    weight = np.where((rows == 0) | (rows == length // 2), 1.0, 2.0) * (rows <= length // 2)
    cosine, sine = trig(shifts % length, rows, length)
    cosine = cosine.astype(ml_dtypes.bfloat16).astype(np.float64)
    sine = sine.astype(ml_dtypes.bfloat16).astype(np.float64)
    return np.concatenate([cosine * weight, -sine * weight], 1).astype(ml_dtypes.bfloat16)


def spin(breadth):
    cosine, sine = trig(np.arange(breadth), np.arange(breadth), breadth)
    forward = np.block([[cosine, -sine], [sine, cosine]])
    back = np.block([[cosine, sine], [-sine, cosine]])
    return np.stack([forward, back]).astype(ml_dtypes.bfloat16)


def table_places(length, breadth):
    sizes = [
        (length // WIDE) * 2 * half_rows(length),
        4 * breadth,
        -(-2 * half_rows(length) // WIDE) * breadth,
        2 * half_rows(breadth),
        breadth,
    ]
    return [(sum(sizes[:k]), size) for k, size in enumerate(sizes)]


def packed_tables(length, breadth):
    def blocks(array):
        rows, columns = array.shape
        array = np.pad(array, ((0, 0), (0, -columns % WIDE)))
        return array.reshape(rows, -1, WIDE).transpose(1, 0, 2).reshape(-1, WIDE)

    parts = [
        forward_table(length),
        spin(breadth).reshape(4 * breadth, 2 * breadth),
        inverse_table(np.arange(breadth) - breadth // 2, length),
        forward_table(breadth),
        inverse_table(np.arange(breadth), breadth),
    ]
    return np.concatenate([blocks(part) for part in parts], 0)


def in_order(q, chunks):
    if isinstance(q, int):
        return (0, chunks - 1, *range(1, chunks - 1))[q]
    return jnp.where(q == 0, 0, jnp.where(q == 1, chunks - 1, q - 1))


def kernel(
    rows, cols, length, breadth,
    strips, occ, tables, out,
    tab, inv_tab, ctab, cinv_tab, spin_v, occ_s, own, got, corner_own, corner_got,
    acc, g_re, g_im, g_inv, z_all, out_v,
    tab_sem, small_sem, own_sem, corner_sem, send_sem, recv_sem,
    csend_sem, crecv_sem, msend_sem, mrecv_sem, out_sem,
):
    chunks = length // CHUNK
    half = half_rows(length)
    chalf = half_rows(breadth)
    row = lax.axis_index("row")
    col = lax.axis_index("col")
    parity = lax.rem(row, 2)
    up, down = lax.rem(row + rows - 1, rows), lax.rem(row + 1, rows)
    left, right = lax.rem(col + cols - 1, cols), lax.rem(col + 1, cols)

    even, odd = parity == 0, parity == 1
    side = jnp.where(even, left, right)
    other_side = jnp.where(even, right, left)
    barrier = pltpu.get_barrier_semaphore()
    neighbours = [
        (row, left), (row, right), (up, col), (down, col), (up, other_side), (down, other_side),
    ]
    for device in neighbours:
        pl.semaphore_signal(barrier, inc=1, device_id=device, device_id_type=MESH)

    places = table_places(length, breadth)
    small = [
        pltpu.make_async_copy(tables.at[pl.ds(*places[k + 1])], dest, small_sem.at[k])
        for k, dest in enumerate((spin_v, inv_tab, ctab, cinv_tab))
    ]
    small.append(pltpu.make_async_copy(occ, occ_s, small_sem.at[4]))
    low = pl.ds(length - breadth, breadth)
    top = pl.ds(0, breadth)
    corner_places = [(0, low), (1, low), (1, top), (0, top)]
    corner_loads = [
        pltpu.make_async_copy(strips.at[s, place], corner_own.at[k], corner_sem.at[k])
        for k, (s, place) in enumerate(corner_places)
    ]
    own_loads = [
        pltpu.make_async_copy(strips.at[2], own.at[0], own_sem.at[0]),
        pltpu.make_async_copy(strips.at[parity], own.at[1], own_sem.at[1]),
    ]

    def table_load(c):
        at = pl.multiple_of(c * (2 * half), 16)
        return pltpu.make_async_copy(
            tables.at[pl.ds(at, 2 * half)], tab.at[c], tab_sem.at[c]
        )

    def start_loads():
        for copy in own_loads[::-1] + small[2:] + small[:2] + corner_loads:
            copy.start()
        for q in range(length // WIDE):
            c = in_order(q // (CHUNK // WIDE), chunks) * (CHUNK // WIDE) + q % (CHUNK // WIDE)
            table_load(c).start()

    pl.semaphore_wait(barrier, len(neighbours))

    def strip_copy(idx, c):
        piece = pl.ds(c * CHUNK if isinstance(c, int) else pl.multiple_of(c * CHUNK, CHUNK), CHUNK)
        source = jnp.where(idx == 0, 3, 1 - parity)
        target = (jnp.where(idx == 0, up, row), jnp.where(idx == 0, col, side))
        return pltpu.make_async_remote_copy(
            src_ref=strips.at[source, piece],
            dst_ref=got.at[idx, piece],
            send_sem=send_sem.at[idx, c],
            recv_sem=recv_sem.at[idx, c],
            device_id=target,
            device_id_type=MESH,
        )

    def corner_copy(k):
        if k < 2:
            source = strips.at[parity, (low, top)[k]]
            target = ((down, up)[k], other_side)
            slot = (2 + parity, 1 - parity)[k]
        else:
            source = got.at[1, (top, low)[k - 2]]
            target = ((up, down)[k - 2], col)
            slot = (parity, 3 - parity)[k - 2]
        return pltpu.make_async_remote_copy(
            src_ref=source,
            dst_ref=corner_got.at[slot],
            send_sem=csend_sem.at[k],
            recv_sem=crecv_sem.at[slot],
            device_id=target,
            device_id_type=MESH,
        )

    def corner_wait(slot):
        pltpu.make_async_remote_copy(
            src_ref=corner_own.at[slot],
            dst_ref=corner_got.at[slot],
            send_sem=csend_sem.at[0],
            recv_sem=crecv_sem.at[slot],
            device_id=(row, left),
            device_id_type=MESH,
        ).wait_recv()

    def send(idx):
        for q in range(chunks):
            strip_copy(idx, in_order(q, chunks)).start()

    def send_corners():
        corner_copy(0).start()
        corner_copy(1).start()

    send(1)
    send_corners()
    pl.when(odd)(lambda: send(0))
    start_loads()

    for copy in small:
        copy.wait()

    def alive(r1, c1, dr, dc):
        r2, c2 = r1 + dr, c1 + dc
        inside = (r2 >= 0) & (r2 < rows) & (c2 >= 0) & (c2 < cols)
        second = occ_s[lax.rem(r2 + rows, rows), lax.rem(c2 + cols, cols)]
        return (occ_s[r1, c1] * second * jnp.where(inside, 1, 0)).astype(F32)


    def cross(c_part, s_part, n, first_row):
        size = c_part.shape[0]
        halves = jnp.concatenate(
            [
                jnp.concatenate([c_part[:, :breadth], s_part[:, :breadth]], 1),
                jnp.concatenate([c_part[:, breadth:], s_part[:, breadth:]], 1),
            ],
            0,
        ).astype(BF16)
        y = jnp.dot(halves, spin_v[: 2 * breadth, :], preferred_element_type=F32).astype(BF16).astype(F32)
        a_re, a_im = y[:size, :breadth], y[:size, breadth:]
        b_re, b_im = y[size:, :breadth], y[size:, breadth:]
        re = a_re * b_re + a_im * b_im
        im = a_im * b_re - a_re * b_im
        square = re * re + im * im
        inverse_m = lax.rsqrt(jnp.maximum(square, 1e-36))
        m = square * inverse_m
        first = lax.broadcasted_iota(jnp.int32, (8, breadth), 0)
        total = jnp.zeros((8, breadth), F32)
        for at in range(0, size, 8):
            part = m[at : at + 8]
            if first_row + at == 0 or first_row + at == n // 2:
                part = part * jnp.where(first == 0, 0.5, 1.0)
            total = total + part
        return re, im, inverse_m, total

    def limit_of(total, n):
        floor = 0.5 * (jnp.sum(total, keepdims=True) * (2.0 / (n * breadth))) + 1e-6
        return 1.0 / floor

    def back(re, im, inverse_m, most, sign):
        scale = jnp.minimum(inverse_m, most)
        r = jnp.concatenate([re * scale, im * (scale * sign)], 1).astype(BF16)
        return jnp.dot(r, spin_v[2 * breadth :, :], preferred_element_type=F32).astype(BF16)

    def edge_map(sign):
        block = half // BLOCKS
        total = jnp.zeros((8, breadth), F32)
        for at in range(0, half, block):
            re, im, inverse_m, part = cross(
                acc[pl.ds(at, block), :], acc[pl.ds(half + at, block), :], length, at
            )
            here = pl.ds(at, block)
            g_re[here, :], g_im[here, :], g_inv[here, :] = re, im, inverse_m
            total = total + part
        most = limit_of(total, length)
        inv = jnp.concatenate(
            [inv_tab[pl.ds(at, breadth), :] for at in range(0, inv_tab.shape[0], breadth)], 1
        )[:, : 2 * half]
        for at in range(0, half, block):
            here = pl.ds(at, block)
            z = back(g_re[here, :], g_im[here, :], g_inv[here, :], most, sign)
            z_all[here, :] = z[:, :breadth]
            z_all[pl.ds(half + at, block), :] = z[:, breadth:]
        return jnp.dot(inv, z_all[...], preferred_element_type=F32)

    def length_step(idx, q, first):
        c = in_order(q, chunks)
        piece = pl.ds(c * CHUNK if isinstance(c, int) else pl.multiple_of(c * CHUNK, CHUNK), CHUNK)

        @pl.when((idx == 0) | (q > 1))
        def _():
            strip_copy(idx, c).wait_recv()

        x = jnp.concatenate([own[idx, piece, :], got[idx, piece, :]], 1)
        step = jnp.concatenate(
            [tab[c * (CHUNK // WIDE) + k] for k in range(CHUNK // WIDE)], 1
        )
        product = jnp.dot(step, x, preferred_element_type=F32)
        if first:
            acc[...] = product
        else:
            acc[...] += product

    def corners():
        scale = 1.0 / math.sqrt(breadth * breadth)
        steps = [(1, 1), (1, -1), (-1, -1), (-1, 1)]
        for k in range(4):
            corner_loads[k].wait()
            corner_wait(k)
        x = jnp.concatenate(
            [part for k in range(4) for part in (corner_own[k], corner_got[k])], 1
        )
        product = jnp.dot(ctab[:, :breadth], x, preferred_element_type=F32)
        parts = []
        for k in range(4):
            wide = product[:, 2 * breadth * k : 2 * breadth * (k + 1)]
            re, im, inverse_m, total = cross(wide[:chalf], wide[chalf:], breadth, 0)
            z = back(re, im, inverse_m, limit_of(total, breadth), 1.0 if k < 2 else -1.0)
            parts.append(jnp.concatenate([z[:, :breadth], z[:, breadth:]], 0))
        maps = jnp.dot(cinv_tab[:, : 2 * chalf], jnp.concatenate(parts, 1), preferred_element_type=F32)
        for k in range(4):
            slot = (2, 3, 6, 7)[k]
            out_v[slot] = (
                maps[:, breadth * k : breadth * (k + 1)] * (alive(row, col, *steps[k]) * scale)
            ).astype(BF16)
            out_copy(slot).start()

    def out_copy(slot):
        return pltpu.make_async_copy(out_v.at[slot], out.at[slot], out_sem.at[slot])

    def map_slots(idx):
        own_slot = jnp.where(idx == 0, 1, 4 * parity)
        return own_slot, jnp.where(idx == 0, 5, 4 - own_slot)

    def map_copy(idx):
        target = (jnp.where(idx == 0, down, row), jnp.where(idx == 0, col, other_side))
        own_slot, far_slot = map_slots(idx)
        return pltpu.make_async_remote_copy(
            src_ref=out_v.at[own_slot],
            dst_ref=out.at[far_slot],
            send_sem=msend_sem.at[idx],
            recv_sem=mrecv_sem.at[idx],
            device_id=target,
            device_id_type=MESH,
        )

    for copy in own_loads:
        copy.wait()

    def hand_on():
        strip_copy(1, 0).wait_recv()
        corner_copy(2).start()
        strip_copy(1, chunks - 1).wait_recv()
        corner_copy(3).start()

    corner_phase = 1
    corner_step = chunks

    def phase(p, carry):
        idx = lax.rem(p + parity, 2)

        pl.when(idx == 1)(hand_on)

        @pl.when(p == 0)
        def _():
            for k in range(CHUNK // WIDE):
                table_load(k).wait()

        length_step(idx, 0, True)


        def more(q, inner):
            @pl.when(p == 0)
            def _():
                for k in range(CHUNK // WIDE):
                    table_load(in_order(q, chunks) * (CHUNK // WIDE) + k).wait()

            @pl.when((p == corner_phase) & (q == corner_step))
            def _():
                corners()

            length_step(idx, q, False)
            pl.when((p == 0) & even & (q == 1))(lambda: send(0))
            return inner

        lax.fori_loop(1, chunks, more, 0)
        sign = jnp.where(idx == 0, 1, 1 - 2 * parity).astype(F32)
        result = edge_map(sign)
        live = alive(
            row, col, jnp.where(idx == 0, 1, 0), jnp.where(idx == 0, 0, 1 - 2 * parity)
        )
        result = result * (live * (1.0 / math.sqrt(length * breadth)))
        slot, _ = map_slots(idx)
        out_v[slot] = result.astype(BF16)
        map_copy(idx).start()
        out_copy(slot).start()
        return carry

    lax.fori_loop(0, 2, phase, 0)
    corners()

    for idx in (1, 0):
        map_copy(idx).wait()

        def sent(c, carry, idx=idx):
            strip_copy(idx, c).wait_send()
            return carry

        lax.fori_loop(0, chunks, sent, 0)
    for k in range(4):
        corner_copy(k).wait_send()
    for slot in (2, 3, 6, 7, 1, 4 * parity):
        out_copy(slot).wait()


def per_device(rows, cols, strips, occupancy):
    length, breadth = strips.shape[4:]
    chunks = length // CHUNK
    half, chalf = half_rows(length), half_rows(breadth)
    tables = jnp.asarray(packed_tables(length, breadth))
    places = table_places(length, breadth)
    hbm = pl.BlockSpec(memory_space=pltpu.HBM)
    dma = pltpu.SemaphoreType.DMA
    result = pl.pallas_call(
        functools.partial(kernel, rows, cols, length, breadth),
        out_shape=jax.ShapeDtypeStruct((8, breadth, breadth), BF16),
        in_specs=[hbm] * 3,
        out_specs=hbm,
        scratch_shapes=[
            pltpu.VMEM((length // WIDE, 2 * half, WIDE), BF16),
            pltpu.VMEM((places[2][1], WIDE), BF16),
            pltpu.VMEM((places[3][1], WIDE), BF16),
            pltpu.VMEM((places[4][1], WIDE), BF16),
            pltpu.VMEM((places[1][1], WIDE), BF16),
            pltpu.SMEM((rows, cols), jnp.int32),
            pltpu.VMEM((2, length, breadth), BF16),
            pltpu.VMEM((2, length, breadth), BF16),
            pltpu.VMEM((4, breadth, breadth), BF16),
            pltpu.VMEM((4, breadth, breadth), BF16),
            pltpu.VMEM((2 * half, 2 * breadth), F32),
            pltpu.VMEM((half, breadth), F32),
            pltpu.VMEM((half, breadth), F32),
            pltpu.VMEM((half, breadth), F32),
            pltpu.VMEM((2 * half, breadth), BF16),
            pltpu.VMEM((8, breadth, breadth), BF16),
            dma((length // WIDE,)),
            dma((5,)),
            dma((2,)),
            dma((4,)),
            dma((2, chunks)),
            dma((2, chunks)),
            dma((4,)),
            dma((4,)),
            dma((2,)),
            dma((2,)),
            dma((8,)),
        ],
        compiler_params=pltpu.CompilerParams(
            collective_id=0, has_side_effects=True, vmem_limit_bytes=54500 * 1024
        ),
    )(strips.reshape(4, length, breadth), occupancy, tables)
    return result.astype(F32)[None, None]


def solution(mesh):
    rows, cols = mesh.shape["row"], mesh.shape["col"]
    return jax.shard_map(
        functools.partial(per_device, rows, cols),
        mesh=mesh,
        in_specs=(P("row", "col", None, None, None, None), P()),
        out_specs=P("row", "col", None, None, None),
        check_vma=False,
    )
```

```python
import functools
import math

import jax
import jax.numpy as jnp
import ml_dtypes
import numpy as np
from jax import lax
from jax.experimental import pallas as pl
from jax.experimental.pallas import tpu as pltpu
from jax.sharding import PartitionSpec as P

MESH = pl.DeviceIdType.MESH
CHUNK = 512
WIDE = 256
BLOCKS = 5
BF16 = jnp.bfloat16
F32 = jnp.float32


def trig(rows, columns, length):
    product = (rows[:, None].astype(np.int64) * columns[None, :]) % length
    angle = (product.astype(np.float32) * np.float32(2.0 * math.pi / length)).astype(np.float64)
    return np.cos(angle), np.sin(angle)


def half_rows(length):
    return -(-(length // 2 + 1) // 16) * 16


def forward_table(length):
    rows = np.arange(half_rows(length))
    cosine, sine = trig(rows, np.arange(length), length)
    keep = (rows <= length // 2)[:, None]
    return np.concatenate([cosine * keep, -sine * keep], 0).astype(ml_dtypes.bfloat16)


def inverse_table(shifts, length):
    rows = np.arange(half_rows(length))
    weight = np.where((rows == 0) | (rows == length // 2), 1.0, 2.0) * (rows <= length // 2)
    cosine, sine = trig(shifts % length, rows, length)
    cosine = cosine.astype(ml_dtypes.bfloat16).astype(np.float64)
    sine = sine.astype(ml_dtypes.bfloat16).astype(np.float64)
    return np.concatenate([cosine * weight, -sine * weight], 1).astype(ml_dtypes.bfloat16)


def spin(breadth):
    cosine, sine = trig(np.arange(breadth), np.arange(breadth), breadth)
    forward = np.block([[cosine, -sine], [sine, cosine]])
    back = np.block([[cosine, sine], [-sine, cosine]])
    return np.stack([forward, back]).astype(ml_dtypes.bfloat16)


def table_places(length, breadth):
    sizes = [
        (length // WIDE) * 2 * half_rows(length),
        4 * breadth,
        -(-2 * half_rows(length) // WIDE) * breadth,
        2 * half_rows(breadth),
        breadth,
    ]
    return [(sum(sizes[:k]), size) for k, size in enumerate(sizes)]


def packed_tables(length, breadth):
    def blocks(array):
        rows, columns = array.shape
        array = np.pad(array, ((0, 0), (0, -columns % WIDE)))
        return array.reshape(rows, -1, WIDE).transpose(1, 0, 2).reshape(-1, WIDE)

    parts = [
        forward_table(length),
        spin(breadth).reshape(4 * breadth, 2 * breadth),
        inverse_table(np.arange(breadth) - breadth // 2, length),
        forward_table(breadth),
        inverse_table(np.arange(breadth), breadth),
    ]
    return np.concatenate([blocks(part) for part in parts], 0)


def in_order(q, chunks):
    if isinstance(q, int):
        return (0, chunks - 1, *range(1, chunks - 1))[q]
    return jnp.where(q == 0, 0, jnp.where(q == 1, chunks - 1, q - 1))


def kernel(
    rows, cols, length, breadth,
    strips, occ, tables, out,
    tab, inv_tab, ctab, cinv_tab, spin_v, occ_s, own, got, corner_own, corner_got,
    acc, g_re, g_im, g_inv, z_all, out_v,
    tab_sem, small_sem, own_sem, corner_sem, send_sem, recv_sem,
    csend_sem, crecv_sem, msend_sem, mrecv_sem, out_sem,
):
    chunks = length // CHUNK
    half = half_rows(length)
    chalf = half_rows(breadth)
    row = lax.axis_index("row")
    col = lax.axis_index("col")
    parity = lax.rem(row, 2)
    up, down = lax.rem(row + rows - 1, rows), lax.rem(row + 1, rows)
    left, right = lax.rem(col + cols - 1, cols), lax.rem(col + 1, cols)

    even, odd = parity == 0, parity == 1
    side = jnp.where(even, left, right)
    other_side = jnp.where(even, right, left)
    barrier = pltpu.get_barrier_semaphore()
    neighbours = [
        (row, left), (row, right), (up, col), (down, col), (up, other_side), (down, other_side),
    ]
    for device in neighbours:
        pl.semaphore_signal(barrier, inc=1, device_id=device, device_id_type=MESH)

    places = table_places(length, breadth)
    small = [
        pltpu.make_async_copy(tables.at[pl.ds(*places[k + 1])], dest, small_sem.at[k])
        for k, dest in enumerate((spin_v, inv_tab, ctab, cinv_tab))
    ]
    small.append(pltpu.make_async_copy(occ, occ_s, small_sem.at[4]))
    low = pl.ds(length - breadth, breadth)
    top = pl.ds(0, breadth)
    corner_places = [(0, low), (1, low), (1, top), (0, top)]
    corner_loads = [
        pltpu.make_async_copy(strips.at[s, place], corner_own.at[k], corner_sem.at[k])
        for k, (s, place) in enumerate(corner_places)
    ]
    own_loads = [
        pltpu.make_async_copy(strips.at[2], own.at[0], own_sem.at[0]),
        pltpu.make_async_copy(strips.at[parity], own.at[1], own_sem.at[1]),
    ]

    def table_load(c):
        at = pl.multiple_of(c * (2 * half), 16)
        return pltpu.make_async_copy(
            tables.at[pl.ds(at, 2 * half)], tab.at[c], tab_sem.at[c]
        )

    def start_loads():
        for copy in own_loads[::-1] + small:
            copy.start()
        for q in range(length // WIDE):
            c = in_order(q // (CHUNK // WIDE), chunks) * (CHUNK // WIDE) + q % (CHUNK // WIDE)
            table_load(c).start()

    pl.semaphore_wait(barrier, len(neighbours))

    def strip_copy(idx, c):
        piece = pl.ds(c * CHUNK if isinstance(c, int) else pl.multiple_of(c * CHUNK, CHUNK), CHUNK)
        source = jnp.where(idx == 0, 3, 1 - parity)
        target = (jnp.where(idx == 0, up, row), jnp.where(idx == 0, col, side))
        return pltpu.make_async_remote_copy(
            src_ref=strips.at[source, piece],
            dst_ref=got.at[idx, piece],
            send_sem=send_sem.at[idx, c],
            recv_sem=recv_sem.at[idx, c],
            device_id=target,
            device_id_type=MESH,
        )

    def corner_copy(k):
        if k < 2:
            source = strips.at[parity, (low, top)[k]]
            target = ((down, up)[k], other_side)
            slot = (2 + parity, 1 - parity)[k]
        else:
            source = got.at[1, (top, low)[k - 2]]
            target = ((up, down)[k - 2], col)
            slot = (parity, 3 - parity)[k - 2]
        return pltpu.make_async_remote_copy(
            src_ref=source,
            dst_ref=corner_got.at[slot],
            send_sem=csend_sem.at[k],
            recv_sem=crecv_sem.at[slot],
            device_id=target,
            device_id_type=MESH,
        )

    def corner_wait(slot):
        pltpu.make_async_remote_copy(
            src_ref=corner_own.at[slot],
            dst_ref=corner_got.at[slot],
            send_sem=csend_sem.at[0],
            recv_sem=crecv_sem.at[slot],
            device_id=(row, left),
            device_id_type=MESH,
        ).wait_recv()

    def send(idx, numbers=None):
        for q in range(chunks) if numbers is None else numbers:
            strip_copy(idx, in_order(q, chunks)).start()

    def send_corners():
        corner_copy(0).start()
        corner_copy(1).start()

    send(1)
    send_corners()
    pl.when(odd)(lambda: send(0))
    start_loads()

    for copy in small:
        copy.wait()

    def alive(r1, c1, dr, dc):
        r2, c2 = r1 + dr, c1 + dc
        inside = (r2 >= 0) & (r2 < rows) & (c2 >= 0) & (c2 < cols)
        second = occ_s[lax.rem(r2 + rows, rows), lax.rem(c2 + cols, cols)]
        return (occ_s[r1, c1] * second * jnp.where(inside, 1, 0)).astype(F32)


    def cross(c_part, s_part, n, first_row):
        size = c_part.shape[0]
        halves = jnp.concatenate(
            [
                jnp.concatenate([c_part[:, :breadth], s_part[:, :breadth]], 1),
                jnp.concatenate([c_part[:, breadth:], s_part[:, breadth:]], 1),
            ],
            0,
        ).astype(BF16)
        y = jnp.dot(halves, spin_v[: 2 * breadth, :], preferred_element_type=F32).astype(BF16).astype(F32)
        a_re, a_im = y[:size, :breadth], y[:size, breadth:]
        b_re, b_im = y[size:, :breadth], y[size:, breadth:]
        re = a_re * b_re + a_im * b_im
        im = a_im * b_re - a_re * b_im
        square = re * re + im * im
        inverse_m = lax.rsqrt(jnp.maximum(square, 1e-36))
        m = square * inverse_m
        first = lax.broadcasted_iota(jnp.int32, (8, breadth), 0)
        total = jnp.zeros((8, breadth), F32)
        for at in range(0, size, 8):
            part = m[at : at + 8]
            if first_row + at == 0 or first_row + at == n // 2:
                part = part * jnp.where(first == 0, 0.5, 1.0)
            total = total + part
        return re, im, inverse_m, total

    def limit_of(total, n):
        floor = 0.5 * (jnp.sum(total, keepdims=True) * (2.0 / (n * breadth))) + 1e-6
        return 1.0 / floor

    def back(re, im, inverse_m, most, sign):
        scale = jnp.minimum(inverse_m, most)
        r = jnp.concatenate([re * scale, im * (scale * sign)], 1).astype(BF16)
        return jnp.dot(r, spin_v[2 * breadth :, :], preferred_element_type=F32).astype(BF16)

    def edge_map(sign):
        block = half // BLOCKS
        total = jnp.zeros((8, breadth), F32)
        for at in range(0, half, block):
            re, im, inverse_m, part = cross(
                acc[pl.ds(at, block), :], acc[pl.ds(half + at, block), :], length, at
            )
            here = pl.ds(at, block)
            g_re[here, :], g_im[here, :], g_inv[here, :] = re, im, inverse_m
            total = total + part
        most = limit_of(total, length)
        inv = jnp.concatenate(
            [inv_tab[pl.ds(at, breadth), :] for at in range(0, inv_tab.shape[0], breadth)], 1
        )[:, : 2 * half]
        for at in range(0, half, block):
            here = pl.ds(at, block)
            z = back(g_re[here, :], g_im[here, :], g_inv[here, :], most, sign)
            z_all[here, :] = z[:, :breadth]
            z_all[pl.ds(half + at, block), :] = z[:, breadth:]
        return jnp.dot(inv, z_all[...], preferred_element_type=F32)

    def length_step(idx, q, first):
        c = in_order(q, chunks)
        piece = pl.ds(c * CHUNK if isinstance(c, int) else pl.multiple_of(c * CHUNK, CHUNK), CHUNK)

        @pl.when((idx == 0) | (q > 1))
        def _():
            strip_copy(idx, c).wait_recv()

        x = jnp.concatenate([own[idx, piece, :], got[idx, piece, :]], 1)
        step = jnp.concatenate(
            [tab[c * (CHUNK // WIDE) + k] for k in range(CHUNK // WIDE)], 1
        )
        product = jnp.dot(step, x, preferred_element_type=F32)
        if first:
            acc[...] = product
        else:
            acc[...] += product

    def corners():
        scale = 1.0 / math.sqrt(breadth * breadth)
        steps = [(1, 1), (1, -1), (-1, -1), (-1, 1)]
        for k in range(4):
            corner_loads[k].wait()
            corner_wait(k)
        x = jnp.concatenate(
            [part for k in range(4) for part in (corner_own[k], corner_got[k])], 1
        )
        product = jnp.dot(ctab[:, :breadth], x, preferred_element_type=F32)
        parts = []
        for k in range(4):
            wide = product[:, 2 * breadth * k : 2 * breadth * (k + 1)]
            re, im, inverse_m, total = cross(wide[:chalf], wide[chalf:], breadth, 0)
            z = back(re, im, inverse_m, limit_of(total, breadth), 1.0 if k < 2 else -1.0)
            parts.append(jnp.concatenate([z[:, :breadth], z[:, breadth:]], 0))
        maps = jnp.dot(cinv_tab[:, : 2 * chalf], jnp.concatenate(parts, 1), preferred_element_type=F32)
        for k in range(4):
            slot = (2, 3, 6, 7)[k]
            out_v[slot] = (
                maps[:, breadth * k : breadth * (k + 1)] * (alive(row, col, *steps[k]) * scale)
            ).astype(BF16)
            out_copy(slot).start()

    def out_copy(slot):
        return pltpu.make_async_copy(out_v.at[slot], out.at[slot], out_sem.at[slot])

    def map_slots(idx):
        own_slot = jnp.where(idx == 0, 1, 4 * parity)
        return own_slot, jnp.where(idx == 0, 5, 4 - own_slot)

    def map_copy(idx):
        target = (jnp.where(idx == 0, down, row), jnp.where(idx == 0, col, other_side))
        own_slot, far_slot = map_slots(idx)
        return pltpu.make_async_remote_copy(
            src_ref=out_v.at[own_slot],
            dst_ref=out.at[far_slot],
            send_sem=msend_sem.at[idx],
            recv_sem=mrecv_sem.at[idx],
            device_id=target,
            device_id_type=MESH,
        )

    for copy in own_loads:
        copy.wait()

    def hand_on():
        strip_copy(1, 0).wait_recv()
        corner_copy(2).start()
        strip_copy(1, chunks - 1).wait_recv()
        corner_copy(3).start()

    corner_phase = 1
    corner_step = chunks

    def phase(p, carry):
        idx = lax.rem(p + parity, 2)

        pl.when(idx == 1)(hand_on)

        @pl.when(p == 0)
        def _():
            for k in range(CHUNK // WIDE):
                table_load(k).wait()

        length_step(idx, 0, True)


        def more(q, inner):
            @pl.when(p == 0)
            def _():
                for k in range(CHUNK // WIDE):
                    table_load(in_order(q, chunks) * (CHUNK // WIDE) + k).wait()

            @pl.when((p == corner_phase) & (q == corner_step))
            def _():
                corners()

            length_step(idx, q, False)
            pl.when((p == 0) & even & (q == 1))(lambda: send(0, (0, 1)))
            pl.when((p == 0) & even & (q == 3))(lambda: send(0, (2, 3)))
            return inner

        lax.fori_loop(1, chunks, more, 0)
        @pl.when(p == 0)
        def _():
            for copy in corner_loads:
                copy.start()

        sign = jnp.where(idx == 0, 1, 1 - 2 * parity).astype(F32)
        result = edge_map(sign)
        live = alive(
            row, col, jnp.where(idx == 0, 1, 0), jnp.where(idx == 0, 0, 1 - 2 * parity)
        )
        result = result * (live * (1.0 / math.sqrt(length * breadth)))
        slot, _ = map_slots(idx)
        out_v[slot] = result.astype(BF16)
        map_copy(idx).start()
        out_copy(slot).start()
        return carry

    lax.fori_loop(0, 2, phase, 0)
    corners()

    for idx in (1, 0):
        map_copy(idx).wait()

        def sent(c, carry, idx=idx):
            strip_copy(idx, c).wait_send()
            return carry

        lax.fori_loop(0, chunks, sent, 0)
    for k in range(4):
        corner_copy(k).wait_send()
    for slot in (2, 3, 6, 7, 1, 4 * parity):
        out_copy(slot).wait()


def per_device(rows, cols, strips, occupancy):
    length, breadth = strips.shape[4:]
    chunks = length // CHUNK
    half, chalf = half_rows(length), half_rows(breadth)
    tables = jnp.asarray(packed_tables(length, breadth))
    places = table_places(length, breadth)
    hbm = pl.BlockSpec(memory_space=pltpu.HBM)
    dma = pltpu.SemaphoreType.DMA
    result = pl.pallas_call(
        functools.partial(kernel, rows, cols, length, breadth),
        out_shape=jax.ShapeDtypeStruct((8, breadth, breadth), BF16),
        in_specs=[hbm] * 3,
        out_specs=hbm,
        scratch_shapes=[
            pltpu.VMEM((length // WIDE, 2 * half, WIDE), BF16),
            pltpu.VMEM((places[2][1], WIDE), BF16),
            pltpu.VMEM((places[3][1], WIDE), BF16),
            pltpu.VMEM((places[4][1], WIDE), BF16),
            pltpu.VMEM((places[1][1], WIDE), BF16),
            pltpu.SMEM((rows, cols), jnp.int32),
            pltpu.VMEM((2, length, breadth), BF16),
            pltpu.VMEM((2, length, breadth), BF16),
            pltpu.VMEM((4, breadth, breadth), BF16),
            pltpu.VMEM((4, breadth, breadth), BF16),
            pltpu.VMEM((2 * half, 2 * breadth), F32),
            pltpu.VMEM((half, breadth), F32),
            pltpu.VMEM((half, breadth), F32),
            pltpu.VMEM((half, breadth), F32),
            pltpu.VMEM((2 * half, breadth), BF16),
            pltpu.VMEM((8, breadth, breadth), BF16),
            dma((length // WIDE,)),
            dma((5,)),
            dma((2,)),
            dma((4,)),
            dma((2, chunks)),
            dma((2, chunks)),
            dma((4,)),
            dma((4,)),
            dma((2,)),
            dma((2,)),
            dma((8,)),
        ],
        compiler_params=pltpu.CompilerParams(
            collective_id=0, has_side_effects=True, vmem_limit_bytes=54500 * 1024
        ),
    )(strips.reshape(4, length, breadth), occupancy, tables)
    return result.astype(F32)[None, None]


def solution(mesh):
    rows, cols = mesh.shape["row"], mesh.shape["col"]
    return jax.shard_map(
        functools.partial(per_device, rows, cols),
        mesh=mesh,
        in_specs=(P("row", "col", None, None, None, None), P()),
        out_specs=P("row", "col", None, None, None),
        check_vma=False,
    )
```

```python
import functools
import math

import jax
import jax.numpy as jnp
import ml_dtypes
import numpy as np
from jax import lax
from jax.experimental import pallas as pl
from jax.experimental.pallas import tpu as pltpu
from jax.sharding import PartitionSpec as P

MESH = pl.DeviceIdType.MESH
CHUNK = 512
WIDE = 256
BLOCKS = 5
BF16 = jnp.bfloat16
F32 = jnp.float32


def trig(rows, columns, length):
    product = (rows[:, None].astype(np.int64) * columns[None, :]) % length
    angle = (product.astype(np.float32) * np.float32(2.0 * math.pi / length)).astype(np.float64)
    return np.cos(angle), np.sin(angle)


def half_rows(length):
    return -(-(length // 2 + 1) // 16) * 16


def forward_table(length):
    rows = np.arange(half_rows(length))
    cosine, sine = trig(rows, np.arange(length), length)
    keep = (rows <= length // 2)[:, None]
    return np.concatenate([cosine * keep, -sine * keep], 0).astype(ml_dtypes.bfloat16)


def inverse_table(shifts, length):
    rows = np.arange(half_rows(length))
    weight = np.where((rows == 0) | (rows == length // 2), 1.0, 2.0) * (rows <= length // 2)
    cosine, sine = trig(shifts % length, rows, length)
    cosine = cosine.astype(ml_dtypes.bfloat16).astype(np.float64)
    sine = sine.astype(ml_dtypes.bfloat16).astype(np.float64)
    return np.concatenate([cosine * weight, -sine * weight], 1).astype(ml_dtypes.bfloat16)


def spin(breadth):
    cosine, sine = trig(np.arange(breadth), np.arange(breadth), breadth)
    forward = np.block([[cosine, -sine], [sine, cosine]])
    back = np.block([[cosine, sine], [-sine, cosine]])
    return np.stack([forward, back]).astype(ml_dtypes.bfloat16)


def table_places(length, breadth):
    sizes = [
        (length // WIDE) * 2 * half_rows(length),
        4 * breadth,
        -(-2 * half_rows(length) // WIDE) * breadth,
        2 * half_rows(breadth),
        breadth,
    ]
    return [(sum(sizes[:k]), size) for k, size in enumerate(sizes)]


def packed_tables(length, breadth):
    def blocks(array):
        rows, columns = array.shape
        array = np.pad(array, ((0, 0), (0, -columns % WIDE)))
        return array.reshape(rows, -1, WIDE).transpose(1, 0, 2).reshape(-1, WIDE)

    parts = [
        forward_table(length),
        spin(breadth).reshape(4 * breadth, 2 * breadth),
        inverse_table(np.arange(breadth) - breadth // 2, length),
        forward_table(breadth),
        inverse_table(np.arange(breadth), breadth),
    ]
    return np.concatenate([blocks(part) for part in parts], 0)


def in_order(q, chunks):
    if isinstance(q, int):
        return (0, chunks - 1, *range(1, chunks - 1))[q]
    return jnp.where(q == 0, 0, jnp.where(q == 1, chunks - 1, q - 1))


def kernel(
    rows, cols, length, breadth,
    strips, occ, tables, out,
    tab, inv_tab, ctab, cinv_tab, spin_v, occ_s, own, got, corner_own, corner_got,
    acc, g_re, g_im, g_inv, z_all, out_v,
    tab_sem, small_sem, own_sem, corner_sem, send_sem, recv_sem,
    csend_sem, crecv_sem, msend_sem, mrecv_sem, out_sem,
):
    chunks = length // CHUNK
    half = half_rows(length)
    chalf = half_rows(breadth)
    row = lax.axis_index("row")
    col = lax.axis_index("col")
    parity = lax.rem(row, 2)
    up, down = lax.rem(row + rows - 1, rows), lax.rem(row + 1, rows)
    left, right = lax.rem(col + cols - 1, cols), lax.rem(col + 1, cols)

    even, odd = parity == 0, parity == 1
    side = jnp.where(even, left, right)
    other_side = jnp.where(even, right, left)
    barrier = pltpu.get_barrier_semaphore()
    neighbours = [
        (row, left), (row, right), (up, col), (down, col), (up, other_side), (down, other_side),
    ]
    for device in neighbours:
        pl.semaphore_signal(barrier, inc=1, device_id=device, device_id_type=MESH)

    places = table_places(length, breadth)
    small = [
        pltpu.make_async_copy(tables.at[pl.ds(*places[k + 1])], dest, small_sem.at[k])
        for k, dest in enumerate((spin_v, inv_tab, ctab, cinv_tab))
    ]
    small.append(pltpu.make_async_copy(occ, occ_s, small_sem.at[4]))
    low = pl.ds(length - breadth, breadth)
    top = pl.ds(0, breadth)
    corner_places = [(0, low), (1, low), (1, top), (0, top)]
    corner_loads = [
        pltpu.make_async_copy(strips.at[s, place], corner_own.at[k], corner_sem.at[k])
        for k, (s, place) in enumerate(corner_places)
    ]
    own_loads = [
        pltpu.make_async_copy(strips.at[2], own.at[0], own_sem.at[0]),
        pltpu.make_async_copy(strips.at[parity], own.at[1], own_sem.at[1]),
    ]

    def table_load(c):
        at = pl.multiple_of(c * (2 * half), 16)
        return pltpu.make_async_copy(
            tables.at[pl.ds(at, 2 * half)], tab.at[c], tab_sem.at[c]
        )

    def start_loads():
        for copy in own_loads[::-1] + small[2:] + small[:2] + corner_loads:
            copy.start()
        for q in range(length // WIDE):
            c = in_order(q // (CHUNK // WIDE), chunks) * (CHUNK // WIDE) + q % (CHUNK // WIDE)
            table_load(c).start()

    pl.semaphore_wait(barrier, len(neighbours))

    def strip_copy(idx, c):
        piece = pl.ds(c * CHUNK if isinstance(c, int) else pl.multiple_of(c * CHUNK, CHUNK), CHUNK)
        source = jnp.where(idx == 0, 3, 1 - parity)
        target = (jnp.where(idx == 0, up, row), jnp.where(idx == 0, col, side))
        return pltpu.make_async_remote_copy(
            src_ref=strips.at[source, piece],
            dst_ref=got.at[idx, piece],
            send_sem=send_sem.at[idx, c],
            recv_sem=recv_sem.at[idx, c],
            device_id=target,
            device_id_type=MESH,
        )

    def corner_copy(k):
        if k < 2:
            source = strips.at[parity, (low, top)[k]]
            target = ((down, up)[k], other_side)
            slot = (2 + parity, 1 - parity)[k]
        else:
            source = got.at[1, (top, low)[k - 2]]
            target = ((up, down)[k - 2], col)
            slot = (parity, 3 - parity)[k - 2]
        return pltpu.make_async_remote_copy(
            src_ref=source,
            dst_ref=corner_got.at[slot],
            send_sem=csend_sem.at[k],
            recv_sem=crecv_sem.at[slot],
            device_id=target,
            device_id_type=MESH,
        )

    def corner_wait(slot):
        pltpu.make_async_remote_copy(
            src_ref=corner_own.at[slot],
            dst_ref=corner_got.at[slot],
            send_sem=csend_sem.at[0],
            recv_sem=crecv_sem.at[slot],
            device_id=(row, left),
            device_id_type=MESH,
        ).wait_recv()

    def send(idx):
        for q in range(chunks):
            strip_copy(idx, in_order(q, chunks)).start()

    def send_corners():
        corner_copy(0).start()
        corner_copy(1).start()

    send(1)
    send_corners()
    pl.when(odd)(lambda: send(0))
    start_loads()

    for copy in small:
        copy.wait()

    def alive(r1, c1, dr, dc):
        r2, c2 = r1 + dr, c1 + dc
        inside = (r2 >= 0) & (r2 < rows) & (c2 >= 0) & (c2 < cols)
        second = occ_s[lax.rem(r2 + rows, rows), lax.rem(c2 + cols, cols)]
        return (occ_s[r1, c1] * second * jnp.where(inside, 1, 0)).astype(F32)


    def cross(c_part, s_part, n, first_row):
        size = c_part.shape[0]
        halves = jnp.concatenate(
            [
                jnp.concatenate([c_part[:, :breadth], s_part[:, :breadth]], 1),
                jnp.concatenate([c_part[:, breadth:], s_part[:, breadth:]], 1),
            ],
            0,
        ).astype(BF16)
        y = jnp.dot(halves, spin_v[: 2 * breadth, :], preferred_element_type=F32).astype(BF16).astype(F32)
        a_re, a_im = y[:size, :breadth], y[:size, breadth:]
        b_re, b_im = y[size:, :breadth], y[size:, breadth:]
        re = a_re * b_re + a_im * b_im
        im = a_im * b_re - a_re * b_im
        square = re * re + im * im
        inverse_m = lax.rsqrt(jnp.maximum(square, 1e-36))
        m = square * inverse_m
        first = lax.broadcasted_iota(jnp.int32, (8, breadth), 0)
        total = jnp.zeros((8, breadth), F32)
        for at in range(0, size, 8):
            part = m[at : at + 8]
            if first_row + at == 0 or first_row + at == n // 2:
                part = part * jnp.where(first == 0, 0.5, 1.0)
            total = total + part
        return re, im, inverse_m, total

    def limit_of(total, n):
        floor = 0.5 * (jnp.sum(total, keepdims=True) * (2.0 / (n * breadth))) + 1e-6
        return 1.0 / floor

    def back(re, im, inverse_m, most, sign):
        scale = jnp.minimum(inverse_m, most)
        r = jnp.concatenate([re * scale, im * (scale * sign)], 1).astype(BF16)
        return jnp.dot(r, spin_v[2 * breadth :, :], preferred_element_type=F32).astype(BF16)

    def edge_map(sign):
        block = half // BLOCKS
        total = jnp.zeros((8, breadth), F32)
        for at in range(0, half, block):
            re, im, inverse_m, part = cross(
                acc[pl.ds(at, block), :], acc[pl.ds(half + at, block), :], length, at
            )
            here = pl.ds(at, block)
            g_re[here, :], g_im[here, :], g_inv[here, :] = re, im, inverse_m
            total = total + part
        most = limit_of(total, length)
        inv = jnp.concatenate(
            [inv_tab[pl.ds(at, breadth), :] for at in range(0, inv_tab.shape[0], breadth)], 1
        )[:, : 2 * half]
        for at in range(0, half, block):
            here = pl.ds(at, block)
            z = back(g_re[here, :], g_im[here, :], g_inv[here, :], most, sign)
            z_all[here, :] = z[:, :breadth]
            z_all[pl.ds(half + at, block), :] = z[:, breadth:]
        return jnp.dot(inv, z_all[...], preferred_element_type=F32)

    def length_step(idx, q, first):
        c = in_order(q, chunks)
        piece = pl.ds(c * CHUNK if isinstance(c, int) else pl.multiple_of(c * CHUNK, CHUNK), CHUNK)

        @pl.when((idx == 0) | (q > 1))
        def _():
            strip_copy(idx, c).wait_recv()

        x = jnp.concatenate([own[idx, piece, :], got[idx, piece, :]], 1)
        step = jnp.concatenate(
            [tab[c * (CHUNK // WIDE) + k] for k in range(CHUNK // WIDE)], 1
        )
        product = jnp.dot(step, x, preferred_element_type=F32)
        if first:
            acc[...] = product
        else:
            acc[...] += product

    def corners():
        scale = 1.0 / math.sqrt(breadth * breadth)
        steps = [(1, 1), (1, -1), (-1, -1), (-1, 1)]
        for k in range(4):
            corner_loads[k].wait()
            corner_wait(k)
        x = jnp.concatenate(
            [part for k in range(4) for part in (corner_own[k], corner_got[k])], 1
        )
        product = jnp.dot(ctab[:, :breadth], x, preferred_element_type=F32)
        parts = []
        for k in range(4):
            wide = product[:, 2 * breadth * k : 2 * breadth * (k + 1)]
            re, im, inverse_m, total = cross(wide[:chalf], wide[chalf:], breadth, 0)
            z = back(re, im, inverse_m, limit_of(total, breadth), 1.0 if k < 2 else -1.0)
            parts.append(jnp.concatenate([z[:, :breadth], z[:, breadth:]], 0))
        maps = jnp.dot(cinv_tab[:, : 2 * chalf], jnp.concatenate(parts, 1), preferred_element_type=F32)
        for k in range(4):
            slot = (2, 3, 6, 7)[k]
            out_v[slot] = (
                maps[:, breadth * k : breadth * (k + 1)] * (alive(row, col, *steps[k]) * scale)
            ).astype(BF16)
            out_copy(slot).start()

    def out_copy(slot):
        return pltpu.make_async_copy(out_v.at[slot], out.at[slot], out_sem.at[slot])

    def map_slots(idx):
        own_slot = jnp.where(idx == 0, 1, 4 * parity)
        return own_slot, jnp.where(idx == 0, 5, 4 - own_slot)

    def map_copy(idx):
        target = (jnp.where(idx == 0, down, row), jnp.where(idx == 0, col, other_side))
        own_slot, far_slot = map_slots(idx)
        return pltpu.make_async_remote_copy(
            src_ref=out_v.at[own_slot],
            dst_ref=out.at[far_slot],
            send_sem=msend_sem.at[idx],
            recv_sem=mrecv_sem.at[idx],
            device_id=target,
            device_id_type=MESH,
        )

    for copy in own_loads:
        copy.wait()

    def hand_on():
        strip_copy(1, 0).wait_recv()
        corner_copy(2).start()
        strip_copy(1, chunks - 1).wait_recv()
        corner_copy(3).start()

    corner_phase = 1
    corner_step = chunks

    def phase(p, carry):
        idx = lax.rem(p + parity, 2)

        pl.when(idx == 1)(hand_on)

        @pl.when(p == 0)
        def _():
            for k in range(CHUNK // WIDE):
                table_load(k).wait()

        length_step(idx, 0, True)


        def more(q, inner):
            @pl.when(p == 0)
            def _():
                for k in range(CHUNK // WIDE):
                    table_load(in_order(q, chunks) * (CHUNK // WIDE) + k).wait()

            @pl.when((p == corner_phase) & (q == corner_step))
            def _():
                corners()

            length_step(idx, q, False)
            pl.when((p == 0) & even & (q == 1 + lax.rem(row // 2, 2)))(lambda: send(0))
            return inner

        lax.fori_loop(1, chunks, more, 0)
        sign = jnp.where(idx == 0, 1, 1 - 2 * parity).astype(F32)
        result = edge_map(sign)
        live = alive(
            row, col, jnp.where(idx == 0, 1, 0), jnp.where(idx == 0, 0, 1 - 2 * parity)
        )
        result = result * (live * (1.0 / math.sqrt(length * breadth)))
        slot, _ = map_slots(idx)
        out_v[slot] = result.astype(BF16)
        map_copy(idx).start()
        out_copy(slot).start()
        return carry

    lax.fori_loop(0, 2, phase, 0)
    corners()

    for idx in (1, 0):
        map_copy(idx).wait()

        def sent(c, carry, idx=idx):
            strip_copy(idx, c).wait_send()
            return carry

        lax.fori_loop(0, chunks, sent, 0)
    for k in range(4):
        corner_copy(k).wait_send()
    for slot in (2, 3, 6, 7, 1, 4 * parity):
        out_copy(slot).wait()


def per_device(rows, cols, strips, occupancy):
    length, breadth = strips.shape[4:]
    chunks = length // CHUNK
    half, chalf = half_rows(length), half_rows(breadth)
    tables = jnp.asarray(packed_tables(length, breadth))
    places = table_places(length, breadth)
    hbm = pl.BlockSpec(memory_space=pltpu.HBM)
    dma = pltpu.SemaphoreType.DMA
    result = pl.pallas_call(
        functools.partial(kernel, rows, cols, length, breadth),
        out_shape=jax.ShapeDtypeStruct((8, breadth, breadth), BF16),
        in_specs=[hbm] * 3,
        out_specs=hbm,
        scratch_shapes=[
            pltpu.VMEM((length // WIDE, 2 * half, WIDE), BF16),
            pltpu.VMEM((places[2][1], WIDE), BF16),
            pltpu.VMEM((places[3][1], WIDE), BF16),
            pltpu.VMEM((places[4][1], WIDE), BF16),
            pltpu.VMEM((places[1][1], WIDE), BF16),
            pltpu.SMEM((rows, cols), jnp.int32),
            pltpu.VMEM((2, length, breadth), BF16),
            pltpu.VMEM((2, length, breadth), BF16),
            pltpu.VMEM((4, breadth, breadth), BF16),
            pltpu.VMEM((4, breadth, breadth), BF16),
            pltpu.VMEM((2 * half, 2 * breadth), F32),
            pltpu.VMEM((half, breadth), F32),
            pltpu.VMEM((half, breadth), F32),
            pltpu.VMEM((half, breadth), F32),
            pltpu.VMEM((2 * half, breadth), BF16),
            pltpu.VMEM((8, breadth, breadth), BF16),
            dma((length // WIDE,)),
            dma((5,)),
            dma((2,)),
            dma((4,)),
            dma((2, chunks)),
            dma((2, chunks)),
            dma((4,)),
            dma((4,)),
            dma((2,)),
            dma((2,)),
            dma((8,)),
        ],
        compiler_params=pltpu.CompilerParams(
            collective_id=0, has_side_effects=True, vmem_limit_bytes=54500 * 1024
        ),
    )(strips.reshape(4, length, breadth), occupancy, tables)
    return result.astype(F32)[None, None]


def solution(mesh):
    rows, cols = mesh.shape["row"], mesh.shape["col"]
    return jax.shard_map(
        functools.partial(per_device, rows, cols),
        mesh=mesh,
        in_specs=(P("row", "col", None, None, None, None), P()),
        out_specs=P("row", "col", None, None, None),
        check_vma=False,
    )
```
